32 devices in a mesh: ctx: 8 (over y, x, core), chan: 4 (over z).
Axes of the slice: x: 2, y: 2, z: 4, core: 2. Of those that a mesh axis runs over, the one named last changes fastest.
Arguments:
- stream: bfloat16 [1024, 8192], P('ctx', 'chan'), may hold values from -64 to 64, as said below
- seg_ids: int32 [1024], P('ctx'), may hold values from 0 to 7, never falling along the last dimension, each value on 1 to 256 neighbouring positions
- mr_gain: float32 [8192], P('chan'), may hold values from 0.1 to 1.9
- mr_filter: bfloat16 [8192, 128], P('chan'), may hold values from -0.5 to 0.5
- li_gain: float32 [8192], P('chan'), may hold values from 0.1 to 1.9
- decay_rates: float32 [8192, 16], P('chan'), may hold values from 0 to 1, as said below
- residues: float32 [8192, 16], P('chan'), may hold values from -1.5 to 1.5
Outputs:
- result: bfloat16 [1024, 8192], P('ctx', 'chan')
The draws below stay inside these ranges and needn't reach their ends.
Inputs may be any that keep to these rules, and one draw needn't show every extreme that they name: `seg_ids`: document numbers never fall along the context; each document holds at most 256 positions, and one holds exactly that many. `stream`: activations. `decay_rates`: positive rates.
All inputs are finite; a program needn't handle non-finite values.
Results may differ from the reference program's by a relative error of at most 0.0064.
Values may be sent and summed in bfloat16 or wider, within the bound.
A program may use at most 128 MiB of HBM per device.

```python
import math
import jax
import jax.numpy as jnp
import numpy as np
from jax import lax

D = 8192
FMR = 128
MODES = 16
DOCS = 8
SEQ = 1024


def draw_stream(key, part):
    key_base, key_cols, key_rows = jax.random.split(key, 3)
    base_values = jnp.clip(jax.random.normal(key_base, (SEQ, D), jnp.float32), -4.0, 4.0)
    rising = jnp.exp(math.log(3.0) * (jnp.arange(D, dtype=jnp.float32) / D - 0.5))
    column_scale = jnp.exp(jax.random.uniform(key_cols, (D,), jnp.float32, minval=math.log(0.3), maxval=math.log(3.0))) * rising
    row_scale = jnp.exp(jax.random.uniform(key_rows, (SEQ, 1), jnp.float32, minval=math.log(0.3), maxval=math.log(3.0)))
    return (base_values * column_scale * row_scale).astype(jnp.bfloat16)


def draw_decay_rates(key, part):
    key_full = jax.random.fold_in(key, 0)
    full_logs = jax.random.uniform(key_full, (D, MODES), jnp.float32, minval=math.log(1.0 / (4.0 * SEQ)), maxval=math.log(1.0 / 30.0))
    return jnp.exp(full_logs)


def level_of(stream_key, shape, pieces, low, high):
    level, own = 1.0, jax.random.fold_in(stream_key, 6)
    for dim, blocks in pieces:
        heights = jnp.exp(jax.random.uniform(jax.random.fold_in(own, dim), (blocks,), jnp.float32, low / len(pieces), high / len(pieces)))
        level = level * jnp.repeat(heights, shape[dim] // blocks).reshape([-1 if axis == dim else 1 for axis in range(len(shape))])
    return level


def length_profile(number_of, total, limit, slope):
    weights = [(1 << 20) // math.isqrt(standing ** slope) + 1 for standing in range(2, number_of + 1)]
    spare, holding = total - limit - (number_of - 1), [1] * (number_of - 1)
    while spare > 0:
        movable = [i for i in range(number_of - 1) if holding[i] < limit]
        mass, left = sum([weights[i] for i in movable]), spare
        for i in movable:
            extra = min(limit - holding[i], max(1, left * weights[i] // mass), spare)
            holding[i] = holding[i] + extra
            spare = spare - extra
    return np.array([limit] + holding)


def ragged(own_key, number_of, total, most, lean):
    if number_of == 2:
        one = jax.random.randint(own_key, (), max(1, total - most), min(most, total - 1) + 1)
        return jnp.stack([one, total - one])
    lengths = jnp.asarray(length_profile(number_of, total, most, lean), jnp.int32)
    twos = (number_of - 1) // 2
    source_of, receiver = lengths[1:1 + 2 * twos:2], lengths[2:2 + 2 * twos:2]
    slack = jnp.minimum(source_of - 1, most - receiver)
    passed = jax.random.randint(jax.random.fold_in(own_key, 1), (twos,), 0, 1 << 20) % (slack + 1)
    lengths = lengths.at[1:1 + 2 * twos:2].set(source_of - passed).at[2:2 + 2 * twos:2].set(receiver + passed)
    return lengths[jax.random.permutation(jax.random.fold_in(own_key, 2), number_of)]


def bell_draw(key, dims, scale, limit, pieces=(), kind=jnp.bfloat16):
    values = jax.random.normal(key, dims, jnp.float32) * scale
    if len(pieces) > 0:
        values = level_of(key, dims, pieces, -0.22, 0.18) * values
    return jnp.clip(values, min=-limit, max=limit).astype(kind)


def setup_inputs(seed: int = 0) -> dict:
    seeds = jax.random.split(jax.random.key(seed), 8)
    stream = draw_stream(jax.random.fold_in(seeds[7], 71), 0)
    seg_ids = jnp.searchsorted(jnp.cumsum(ragged(seeds[1], DOCS, SEQ, SEQ // 4, 2)), jnp.arange(SEQ), side="right").astype(jnp.int32)
    mr_gain = jnp.clip(1.0 + 0.18 * jax.random.normal(seeds[2], (D,), jnp.float32), 0.1, 1.9)
    mr_filter = bell_draw(seeds[3], (D, FMR), FMR ** -0.5, 0.5, ((0, 4),))
    li_gain = jnp.clip(1.0 + 0.18 * jax.random.normal(seeds[4], (D,), jnp.float32), 0.1, 1.9)
    decay_rates = draw_decay_rates(jax.random.fold_in(seeds[7], 71), 0)
    residues = bell_draw(seeds[6], (D, MODES), MODES ** -0.5, 1.5, ((0, 4),), jnp.float32)
    return dict(stream=stream, seg_ids=seg_ids, mr_gain=mr_gain, mr_filter=mr_filter, li_gain=li_gain, decay_rates=decay_rates, residues=residues)


EPSILON = 1e-06

def depthwise(widened, filter_taps):
    rim_rows = filter_taps.shape[1] - 1
    count = widened.shape[0] - rim_rows
    taps_float = filter_taps.astype(jnp.float32)
    total = jnp.zeros((count, filter_taps.shape[0]), jnp.float32)
    for lag in range(rim_rows + 1):
        rows = widened[rim_rows - lag:rim_rows - lag + count].astype(jnp.float32)
        total = total + rows * taps_float[:, lag]
    return total

def reference(stream, seg_ids, mr_gain, mr_filter, li_gain, decay_rates, residues):
    rim_rows = FMR - 1
    xfloat = stream.astype(jnp.float32)
    inverse = lax.rsqrt(lax.optimization_barrier(jnp.mean(xfloat * xfloat, axis=1, keepdims=True)) + EPSILON)
    normed = (xfloat * inverse * mr_gain).astype(jnp.bfloat16)
    widened = jnp.concatenate([jnp.zeros((rim_rows, D), jnp.bfloat16), normed])
    mixed = depthwise(widened, mr_filter)
    first = (xfloat + normed.astype(jnp.float32) * mixed).astype(jnp.bfloat16)
    first_float = first.astype(jnp.float32)
    inverse_two = lax.rsqrt(lax.optimization_barrier(jnp.mean(first_float * first_float, axis=1, keepdims=True)) + EPSILON)
    second = first_float * inverse_two * li_gain
    decays = jnp.exp(-decay_rates)
    coefs = residues * jnp.sqrt(-jnp.expm1(-2.0 * decay_rates))
    keeps = jnp.concatenate([jnp.zeros((1,), jnp.float32), (seg_ids[1:] == seg_ids[:-1]).astype(jnp.float32)])

    def advance(state, inputs):
        keep_flag, row_values = inputs
        state = keep_flag * decays * state + row_values[:, None]
        return (state, lax.optimization_barrier(jnp.sum(coefs * state, axis=1)))
    final_state, longconv = lax.scan(advance, jnp.zeros((D, MODES), jnp.float32), (keeps, second))
    return (first_float + second * longconv).astype(jnp.bfloat16)
```

```python
from functools import partial

import jax
import jax.numpy as jnp
import numpy as np
from jax import lax
from jax.experimental import pallas as pl
from jax.experimental.pallas import tpu as pltpu
from jax.sharding import PartitionSpec as P

EPSILON = 1e-06
MESH = pl.DeviceIdType.MESH
F32 = jnp.float32
BF16 = jnp.bfloat16
UNROLL = 4


def split_table(table):
    high = table.astype(BF16)
    low = (table - high.astype(np.float64)).astype(BF16)
    return high, low


def dft_tables(rows):
    size = 2 * rows
    k = np.arange(rows)[:, None] + 0.5
    n = np.arange(size)[None, :]
    angle = 2.0 * np.pi * k * n / size
    forward = np.concatenate([np.cos(angle), -np.sin(angle)])
    inverse = (2.0 / size) * forward[:, rows:].T
    return split_table(forward) + split_table(inverse)


def split(x):
    high = x.astype(BF16)
    return high, (x - high.astype(F32)).astype(BF16)


def mm(a, b):
    return jnp.dot(a, b, preferred_element_type=F32)


def mm_nt(a, b):
    return lax.dot_general(a, b, (((1,), (1,)), ((), ())), preferred_element_type=F32)


def kernel(
    n_ctx, n_chan, look, width,
    stream, seg, gain1, taps, gain2, rates, residues, fh, fl, gh, gl,
    out,
    halo, ext, spec, first, xs, ys, dsl, csl, keepb, aliveb,
    part1, part2, sums1, sums2, invs, invr, idb, idr, ends, endr,
    halo_s, halo_r, p1_s, p1_r, p2_s, p2_r, inv_s, inv_r, id_s, id_r, end_s, end_r,
):
    rows, channels = stream.shape
    modes = rates.shape[0]
    chunk = min(256, channels)
    chunks = channels // chunk
    tiles = channels // 128
    group = min(8, tiles)
    halves = tiles // group
    k = lax.axis_index("ctx")
    z = lax.axis_index("chan")

    barrier = pltpu.get_barrier_semaphore()

    def peer(r):
        return {"chan": lax.rem(z + r, n_chan)}

    for r in range(1, n_chan):
        pl.semaphore_signal(barrier, inc=1, device_id=peer(r), device_id_type=MESH)
    for i in range(1, look + 1):
        @pl.when(k + i < n_ctx)
        def _():
            pl.semaphore_signal(barrier, inc=1, device_id={"ctx": k + i}, device_id_type=MESH)

        @pl.when(k >= i)
        def _():
            pl.semaphore_signal(barrier, inc=1, device_id={"ctx": k - i}, device_id_type=MESH)

    eye = lax.broadcasted_iota(jnp.int32, (rows, rows), 0) == lax.broadcasted_iota(
        jnp.int32, (rows, rows), 1
    )

    def to_col(row):
        return jnp.sum(jnp.where(eye, row, 0.0), axis=1, keepdims=True)

    def to_row(col):
        return jnp.sum(jnp.where(eye, col, 0.0), axis=0, keepdims=True)

    def square_step(j, acc):
        x = stream[:, pl.ds(pl.multiple_of(j * 128, 128), 128)].astype(F32)
        return acc + x * x

    acc = lax.fori_loop(0, tiles, square_step, jnp.zeros((rows, 128), F32), unroll=True)
    row = to_row(jnp.sum(acc, axis=1, keepdims=True))
    part1[...] = jnp.broadcast_to(row, part1.shape)
    segf = seg[...].astype(F32)
    lanes = lax.broadcasted_iota(jnp.int32, (1, rows), 1)
    last = jnp.sum(jnp.where(lanes == rows - 1, segf, 0.0), axis=1, keepdims=True)
    idb[...] = jnp.broadcast_to(last, idb.shape)

    peers = n_chan - 1 + jnp.minimum(k, look) + jnp.minimum(n_ctx - 1 - k, look)
    pl.semaphore_wait(barrier, peers)

    def copy(src, dst, s, r, where):
        return pltpu.make_async_remote_copy(
            src_ref=src, dst_ref=dst, send_sem=s, recv_sem=r, device_id=where, device_id_type=MESH
        )

    def sum_copy(part, sums, s, r, i):
        return copy(part, sums.at[i - 1], s.at[i - 1], r.at[i - 1], peer(i))

    def halo_copy(q):
        cols = pl.ds(pl.multiple_of(q * chunk, chunk), chunk)
        return copy(
            stream.at[:, cols], halo.at[:, cols], halo_s.at[q], halo_r.at[q], {"ctx": k + 1}
        )

    def id_copy(i):
        return copy(idb, idr.at[i - 1], id_s.at[i - 1], id_r.at[i - 1], {"ctx": k + i})

    def end_copy(i, h):
        e = (i - 1) * halves + h
        return copy(ends.at[h], endr.at[e], end_s.at[e], end_r.at[e], {"ctx": k + i})

    inv_copy = copy(invs, invr, inv_s, inv_r, {"ctx": k + 1})

    for i in range(1, n_chan):
        sum_copy(part1, sums1, p1_s, p1_r, i).start()

    @pl.when(k + 1 < n_ctx)
    def _():
        for q in range(chunks):
            halo_copy(q).start()

    for i in range(1, look + 1):
        @pl.when(k + i < n_ctx)
        def _():
            id_copy(i).start()

    def spectrum_step(q, c):
        at = pl.ds(pl.multiple_of(q * chunk, chunk), chunk)
        h = taps[at, :]
        spec[:, at] = mm_nt(fh[:, :rows], h) + mm_nt(fl[:, :rows], h)
        return c

    lax.fori_loop(0, chunks, spectrum_step, 0)

    for j in range(tiles):
        at = slice(j * 128, (j + 1) * 128)
        rate = rates[:, at]
        dsl[j * modes : (j + 1) * modes, :] = jnp.exp(-rate)
        doubled = 2.0 * rate
        small = doubled * (1.0 - doubled * (0.5 - doubled * (1.0 / 6.0 - doubled * (1.0 / 24.0 - doubled * (1.0 / 120.0)))))
        gap = jnp.where(doubled < 0.05, small, 1.0 - jnp.exp(-doubled))
        csl[j * modes : (j + 1) * modes, :] = residues[:, at] * jnp.sqrt(gap)
    seg_col = to_col(segf)
    before = lax.broadcasted_iota(jnp.int32, (rows, rows), 0) - 1 == lax.broadcasted_iota(
        jnp.int32, (rows, rows), 1
    )
    prev_col = jnp.sum(jnp.where(before, segf, 0.0), axis=1, keepdims=True)
    keepb[...] = jnp.broadcast_to(jnp.where(seg_col == prev_col, 1.0, 0.0), keepb.shape)

    for i in range(1, n_chan):
        sum_copy(part1, sums1, p1_s, p1_r, i).wait_recv()
    total = part1[...]
    for i in range(1, n_chan):
        total = total + sums1[i - 1]
    full = channels * n_chan
    inverse = lax.rsqrt(total / full + EPSILON)
    invs[...] = inverse

    @pl.when(k + 1 < n_ctx)
    def _():
        inv_copy.start()

    inv_col = to_col(inverse[0:1, :])

    def norm_step(q, c):
        at = pl.ds(pl.multiple_of(q * chunk, chunk), chunk)
        ext[rows:, at] = (stream[:, at].astype(F32) * inv_col * gain1[:, at]).astype(BF16)
        return c

    lax.fori_loop(0, chunks, norm_step, 0)

    @pl.when(k > 0)
    def _():
        inv_copy.wait_recv()

    @pl.when(k == 0)
    def _():
        halo[...] = jnp.zeros_like(halo)
        invr[...] = jnp.zeros_like(invr)

    halo_col = to_col(invr[0:1, :])

    def conv_step(q, acc):
        @pl.when(k > 0)
        def _():
            halo_copy(q).wait_recv()

        at = pl.ds(pl.multiple_of(q * chunk, chunk), chunk)
        ext[:rows, at] = (halo[:, at].astype(F32) * halo_col * gain1[:, at]).astype(BF16)
        x = ext[:, at]
        freq = mm(fh[...], x) + mm(fl[...], x)
        h = spec[:, at]
        xr, xi, hr, hi = freq[:rows], freq[rows:], h[:rows], h[rows:]
        prod = jnp.concatenate([xr * hr - xi * hi, xr * hi + xi * hr], axis=0)
        ph, plow = split(prod)
        mixed = mm(gh[...], ph) + mm(gh[...], plow) + mm(gl[...], ph)
        one = stream[:, at].astype(F32) + x[rows:].astype(F32) * mixed
        one = one.astype(BF16)
        first[:, at] = one
        one = one.astype(F32)
        sq = one * one
        for s in range(chunk // 128):
            acc = acc + sq[:, s * 128 : (s + 1) * 128]
        return acc

    acc = lax.fori_loop(0, chunks, conv_step, jnp.zeros((rows, 128), F32))
    row = to_row(jnp.sum(acc, axis=1, keepdims=True))
    part2[...] = jnp.broadcast_to(row, part2.shape)
    for i in range(1, n_chan):
        sum_copy(part2, sums2, p2_s, p2_r, i).start()
    for i in range(1, look + 1):
        @pl.when(k >= i)
        def _():
            id_copy(i).wait_recv()

    @pl.when(k > 0)
    def _():
        q = idr[0]
        aliveb[...] = jnp.where(seg_col == q[0:1, :], 1.0, 0.0)

    for i in range(1, n_chan):
        sum_copy(part2, sums2, p2_s, p2_r, i).wait_recv()
    total = part2[...]
    for i in range(1, n_chan):
        total = total + sums2[i - 1]
    inv2_col = to_col(lax.rsqrt(total / full + EPSILON)[0:1, :])

    for j in range(tiles):
        at = slice(j * 128, (j + 1) * 128)
        xs[j * rows : (j + 1) * rows, :] = first[:, at].astype(F32) * inv2_col * gain2[:, at]

    def coef_rows(ref, h, m):
        return ref[pl.ds(h * group * modes + m, group, stride=modes), :]

    def time_rows(h, t):
        return pl.ds(h * group * rows + t, group, stride=rows)

    def tree(terms):
        while len(terms) > 1:
            terms = [a + b for a, b in zip(terms[::2], terms[1::2])] + (
                [terms[-1]] if len(terms) % 2 else []
            )
        return terms[0]

    for h in range(halves):
        d = [coef_rows(dsl, h, m) for m in range(modes)]
        c = [coef_rows(csl, h, m) for m in range(modes)]

        def step(b, state):
            for u in range(UNROLL):
                t = b * UNROLL + u
                x = xs[time_rows(h, t), :]
                keep = jnp.broadcast_to(keepb[pl.ds(t, 1), :], x.shape)
                state = [(keep * s) * dm + x for s, dm in zip(state, d)]
                ys[time_rows(h, t), :] = tree([cm * s for cm, s in zip(c, state)])
            return state

        state = lax.fori_loop(0, rows // UNROLL, step, [jnp.zeros((group, 128), F32)] * modes)
        ends[h] = jnp.concatenate(state, axis=0).astype(BF16)
        for i in range(1, look + 1):
            @pl.when(k + i < n_ctx)
            def _():
                end_copy(i, h).start()

    for h in range(halves):
        for i in range(1, look + 1):
            @pl.when(k >= i)
            def _():
                end_copy(i, h).wait_recv()

        @pl.when(k > 0)
        def _():
            d = [coef_rows(dsl, h, m) for m in range(modes)]
            c = [coef_rows(csl, h, m) for m in range(modes)]
            entering = endr[h].astype(F32)
            carried = [entering[m * group : (m + 1) * group] for m in range(modes)]
            powers = list(d)
            hops = 1
            while hops < rows:
                powers = [p * p for p in powers]
                hops *= 2
            decay = powers
            for i in range(2, look + 1):
                same = jnp.where(idr[i - 1] == idr[0], 1.0, 0.0)[:group]
                same = jnp.where(k >= i, same, 0.0)
                old = endr[(i - 1) * halves + h].astype(F32)
                carried = [
                    a + jnp.where(same > 0.0, p * old[m * group : (m + 1) * group], 0.0)
                    for m, (a, p) in enumerate(zip(carried, decay))
                ]
                decay = [p * q for p, q in zip(decay, powers)]
            lead = [cm * dm * s for cm, dm, s in zip(c, d, carried)]

            def step(b, lead):
                for u in range(UNROLL):
                    t = b * UNROLL + u
                    at = time_rows(h, t)
                    alive = jnp.broadcast_to(aliveb[pl.ds(t, 1), :], (group, 128))
                    ys[at, :] = ys[at, :] + alive * tree(lead)
                    lead = [p * dm for p, dm in zip(lead, d)]
                return lead

            lax.fori_loop(0, rows // UNROLL, step, lead)

        for j in range(h * group, (h + 1) * group):
            at = slice(j * 128, (j + 1) * 128)
            slab = slice(j * rows, (j + 1) * rows)
            out[:, at] = (first[:, at].astype(F32) + xs[slab, :] * ys[slab, :]).astype(BF16)

    for i in range(1, n_chan):
        sum_copy(part1, sums1, p1_s, p1_r, i).wait_send()
        sum_copy(part2, sums2, p2_s, p2_r, i).wait_send()

    @pl.when(k + 1 < n_ctx)
    def _():
        inv_copy.wait_send()
        for q in range(chunks):
            halo_copy(q).wait_send()

    for i in range(1, look + 1):
        @pl.when(k + i < n_ctx)
        def _():
            id_copy(i).wait_send()
            for h in range(halves):
                end_copy(i, h).wait_send()


def per_device(stream, seg_ids, mr_gain, mr_filter, li_gain, decay_rates, residues):
    rows, channels = stream.shape
    modes = decay_rates.shape[1]
    n_ctx, n_chan = lax.axis_size("ctx"), lax.axis_size("chan")
    assert rows == mr_filter.shape[1]
    longest = rows * n_ctx // 4
    look = max(1, min(n_ctx - 1, -(-(longest - 1) // rows)))
    tiles = channels // 128
    group = min(8, tiles)
    halves = tiles // group
    chunks = channels // min(256, channels)
    vmem = pl.BlockSpec(memory_space=pltpu.VMEM)
    dma = pltpu.SemaphoreType.DMA
    others = max(1, n_chan - 1)
    small = (8, 128)
    tables = [jnp.asarray(t) for t in dft_tables(rows)]
    return pl.pallas_call(
        partial(kernel, n_ctx, n_chan, look, channels),
        out_shape=jax.ShapeDtypeStruct((rows, channels), BF16),
        in_specs=[vmem] * 11,
        out_specs=vmem,
        scratch_shapes=[
            pltpu.VMEM((rows, channels), BF16),
            pltpu.VMEM((2 * rows, channels), BF16),
            pltpu.VMEM((2 * rows, channels), F32),
            pltpu.VMEM((rows, channels), BF16),
            pltpu.VMEM((tiles * rows, 128), F32),
            pltpu.VMEM((tiles * rows, 128), F32),
            pltpu.VMEM((tiles * modes, 128), F32),
            pltpu.VMEM((tiles * modes, 128), F32),
            pltpu.VMEM((rows, 128), F32),
            pltpu.VMEM((rows, 128), F32),
            pltpu.VMEM(small, F32),
            pltpu.VMEM(small, F32),
            pltpu.VMEM((others,) + small, F32),
            pltpu.VMEM((others,) + small, F32),
            pltpu.VMEM(small, F32),
            pltpu.VMEM(small, F32),
            pltpu.VMEM(small, F32),
            pltpu.VMEM((look,) + small, F32),
            pltpu.VMEM((halves, modes * group, 128), BF16),
            pltpu.VMEM((look * halves, modes * group, 128), BF16),
            dma((chunks,)), dma((chunks,)),
            dma((others,)), dma((others,)),
            dma((others,)), dma((others,)),
            dma, dma,
            dma((look,)), dma((look,)),
            dma((look * halves,)), dma((look * halves,)),
        ],
        compiler_params=pltpu.CompilerParams(
            collective_id=0, has_side_effects=True, vmem_limit_bytes=40 * 2**20
        ),
    )(
        stream, seg_ids.reshape(1, rows), mr_gain.reshape(1, channels), mr_filter,
        li_gain.reshape(1, channels), decay_rates.T, residues.T, *tables,
    )


def solution(mesh):
    placed = (
        P("ctx", "chan"),
        P("ctx"),
        P("chan"),
        P("chan", None),
        P("chan"),
        P("chan", None),
        P("chan", None),
    )
    return jax.shard_map(
        per_device, mesh=mesh, in_specs=placed, out_specs=P("ctx", "chan"), check_vma=False
    )
```

```python
from functools import partial

import jax
import jax.numpy as jnp
import numpy as np
from jax import lax
from jax.experimental import pallas as pl
from jax.experimental.pallas import tpu as pltpu
from jax.sharding import PartitionSpec as P

EPSILON = 1e-06
MESH = pl.DeviceIdType.MESH
F32 = jnp.float32
BF16 = jnp.bfloat16
UNROLL = 4


def split_table(table):
    high = table.astype(BF16)
    low = (table - high.astype(np.float64)).astype(BF16)
    return high, low


def dft_tables(rows):
    size = 2 * rows
    k = np.arange(rows)[:, None] + 0.5
    n = np.arange(size)[None, :]
    angle = 2.0 * np.pi * k * n / size
    forward = np.concatenate([np.cos(angle), -np.sin(angle)])
    inverse = (2.0 / size) * forward[:, rows:].T
    return split_table(forward) + split_table(inverse)


def split(x):
    high = x.astype(BF16)
    return high, (x - high.astype(F32)).astype(BF16)


def mm(a, b):
    return jnp.dot(a, b, preferred_element_type=F32)


def mm_nt(a, b):
    return lax.dot_general(a, b, (((1,), (1,)), ((), ())), preferred_element_type=F32)


def kernel(
    n_ctx, n_chan, look, width,
    *refs,
):
    sources, out, held, load_sem = refs[:11], refs[11], refs[12:23], refs[23]
    (
        halo, ext, spec, first, xs, ys, dsl, csl, keepb, aliveb,
        part1, part2, sums1, sums2, invs, invr, idb, idr, ends, endr,
        halo_s, halo_r, p1_s, p1_r, p2_s, p2_r, inv_s, inv_r, id_s, id_r, end_s, end_r,
    ) = refs[24:]
    stream, seg, gain1, taps, gain2, rates, residues, fh, fl, gh, gl = held
    loads = [
        pltpu.make_async_copy(source, target, load_sem.at[i])
        for i, (source, target) in enumerate(zip(sources, held))
    ]
    for i in (0, 1, 7, 8, 3, 5, 6, 2, 9, 10, 4):
        loads[i].start()
    rows, channels = stream.shape
    modes = rates.shape[0]
    chunk = min(256, channels)
    chunks = channels // chunk
    tiles = channels // 128
    group = min(8, tiles)
    halves = tiles // group
    k = lax.axis_index("ctx")
    z = lax.axis_index("chan")

    barrier = pltpu.get_barrier_semaphore()

    def peer(r):
        return {"chan": lax.rem(z + r, n_chan)}

    for r in range(1, n_chan):
        pl.semaphore_signal(barrier, inc=1, device_id=peer(r), device_id_type=MESH)
    for i in range(1, look + 1):
        @pl.when(k + i < n_ctx)
        def _():
            pl.semaphore_signal(barrier, inc=1, device_id={"ctx": k + i}, device_id_type=MESH)

        @pl.when(k >= i)
        def _():
            pl.semaphore_signal(barrier, inc=1, device_id={"ctx": k - i}, device_id_type=MESH)

    eye = lax.broadcasted_iota(jnp.int32, (rows, rows), 0) == lax.broadcasted_iota(
        jnp.int32, (rows, rows), 1
    )

    def to_col(row):
        return jnp.sum(jnp.where(eye, row, 0.0), axis=1, keepdims=True)

    def to_row(col):
        return jnp.sum(jnp.where(eye, col, 0.0), axis=0, keepdims=True)

    loads[0].wait()
    loads[1].wait()

    def square_step(j, acc):
        x = stream[:, pl.ds(pl.multiple_of(j * 128, 128), 128)].astype(F32)
        return acc + x * x

    acc = lax.fori_loop(0, tiles, square_step, jnp.zeros((rows, 128), F32), unroll=True)
    row = to_row(jnp.sum(acc, axis=1, keepdims=True))
    part1[...] = jnp.broadcast_to(row, part1.shape)
    segf = seg[...].astype(F32)
    lanes = lax.broadcasted_iota(jnp.int32, (1, rows), 1)
    last = jnp.sum(jnp.where(lanes == rows - 1, segf, 0.0), axis=1, keepdims=True)
    idb[...] = jnp.broadcast_to(last, idb.shape)

    peers = n_chan - 1 + jnp.minimum(k, look) + jnp.minimum(n_ctx - 1 - k, look)
    pl.semaphore_wait(barrier, peers)

    def copy(src, dst, s, r, where):
        return pltpu.make_async_remote_copy(
            src_ref=src, dst_ref=dst, send_sem=s, recv_sem=r, device_id=where, device_id_type=MESH
        )

    def sum_copy(part, sums, s, r, i):
        return copy(part, sums.at[i - 1], s.at[i - 1], r.at[i - 1], peer(i))

    def halo_copy(q):
        cols = pl.ds(pl.multiple_of(q * chunk, chunk), chunk)
        return copy(
            sources[0].at[:, cols], halo.at[:, cols], halo_s.at[q], halo_r.at[q], {"ctx": k + 1}
        )

    def id_copy(i):
        return copy(idb, idr.at[i - 1], id_s.at[i - 1], id_r.at[i - 1], {"ctx": k + i})

    def end_copy(i, h):
        e = (i - 1) * halves + h
        return copy(ends.at[h], endr.at[e], end_s.at[e], end_r.at[e], {"ctx": k + i})

    inv_copy = copy(invs, invr, inv_s, inv_r, {"ctx": k + 1})

    for i in range(1, n_chan):
        sum_copy(part1, sums1, p1_s, p1_r, i).start()

    @pl.when(k + 1 < n_ctx)
    def _():
        for q in range(chunks):
            halo_copy(q).start()

    for i in range(1, look + 1):
        @pl.when(k + i < n_ctx)
        def _():
            id_copy(i).start()

    for i in (7, 8, 3):
        loads[i].wait()

    def spectrum_step(q, c):
        at = pl.ds(pl.multiple_of(q * chunk, chunk), chunk)
        h = taps[at, :]
        spec[:, at] = mm_nt(fh[:, :rows], h) + mm_nt(fl[:, :rows], h)
        return c

    lax.fori_loop(0, chunks, spectrum_step, 0)

    for i in (5, 6, 2, 9, 10, 4):
        loads[i].wait()

    for j in range(tiles):
        at = slice(j * 128, (j + 1) * 128)
        rate = rates[:, at]
        dsl[j * modes : (j + 1) * modes, :] = jnp.exp(-rate)
        doubled = 2.0 * rate
        small = doubled * (1.0 - doubled * (0.5 - doubled * (1.0 / 6.0 - doubled * (1.0 / 24.0 - doubled * (1.0 / 120.0)))))
        gap = jnp.where(doubled < 0.05, small, 1.0 - jnp.exp(-doubled))
        csl[j * modes : (j + 1) * modes, :] = residues[:, at] * jnp.sqrt(gap)
    seg_col = to_col(segf)
    before = lax.broadcasted_iota(jnp.int32, (rows, rows), 0) - 1 == lax.broadcasted_iota(
        jnp.int32, (rows, rows), 1
    )
    prev_col = jnp.sum(jnp.where(before, segf, 0.0), axis=1, keepdims=True)
    keepb[...] = jnp.broadcast_to(jnp.where(seg_col == prev_col, 1.0, 0.0), keepb.shape)

    for i in range(1, n_chan):
        sum_copy(part1, sums1, p1_s, p1_r, i).wait_recv()
    total = part1[...]
    for i in range(1, n_chan):
        total = total + sums1[i - 1]
    full = channels * n_chan
    inverse = lax.rsqrt(total / full + EPSILON)
    invs[...] = inverse

    @pl.when(k + 1 < n_ctx)
    def _():
        inv_copy.start()

    inv_col = to_col(inverse[0:1, :])

    def norm_step(q, c):
        at = pl.ds(pl.multiple_of(q * chunk, chunk), chunk)
        ext[rows:, at] = (stream[:, at].astype(F32) * inv_col * gain1[:, at]).astype(BF16)
        return c

    lax.fori_loop(0, chunks, norm_step, 0)

    @pl.when(k > 0)
    def _():
        inv_copy.wait_recv()

    @pl.when(k == 0)
    def _():
        halo[...] = jnp.zeros_like(halo)
        invr[...] = jnp.zeros_like(invr)

    halo_col = to_col(invr[0:1, :])

    def conv_step(q, acc):
        @pl.when(k > 0)
        def _():
            halo_copy(q).wait_recv()

        at = pl.ds(pl.multiple_of(q * chunk, chunk), chunk)
        ext[:rows, at] = (halo[:, at].astype(F32) * halo_col * gain1[:, at]).astype(BF16)
        x = ext[:, at]
        freq = mm(fh[...], x) + mm(fl[...], x)
        h = spec[:, at]
        xr, xi, hr, hi = freq[:rows], freq[rows:], h[:rows], h[rows:]
        prod = jnp.concatenate([xr * hr - xi * hi, xr * hi + xi * hr], axis=0)
        ph, plow = split(prod)
        mixed = mm(gh[...], ph) + mm(gh[...], plow) + mm(gl[...], ph)
        one = stream[:, at].astype(F32) + x[rows:].astype(F32) * mixed
        one = one.astype(BF16)
        first[:, at] = one
        one = one.astype(F32)
        sq = one * one
        for s in range(chunk // 128):
            acc = acc + sq[:, s * 128 : (s + 1) * 128]
        return acc

    acc = lax.fori_loop(0, chunks, conv_step, jnp.zeros((rows, 128), F32))
    row = to_row(jnp.sum(acc, axis=1, keepdims=True))
    part2[...] = jnp.broadcast_to(row, part2.shape)
    for i in range(1, n_chan):
        sum_copy(part2, sums2, p2_s, p2_r, i).start()
    for i in range(1, look + 1):
        @pl.when(k >= i)
        def _():
            id_copy(i).wait_recv()

    @pl.when(k > 0)
    def _():
        q = idr[0]
        aliveb[...] = jnp.where(seg_col == q[0:1, :], 1.0, 0.0)

    for i in range(1, n_chan):
        sum_copy(part2, sums2, p2_s, p2_r, i).wait_recv()
    total = part2[...]
    for i in range(1, n_chan):
        total = total + sums2[i - 1]
    inv2_col = to_col(lax.rsqrt(total / full + EPSILON)[0:1, :])

    for j in range(tiles):
        at = slice(j * 128, (j + 1) * 128)
        xs[j * rows : (j + 1) * rows, :] = first[:, at].astype(F32) * inv2_col * gain2[:, at]

    def coef_rows(ref, h, m):
        return ref[pl.ds(h * group * modes + m, group, stride=modes), :]

    def time_rows(h, t):
        return pl.ds(h * group * rows + t, group, stride=rows)

    def tree(terms):
        while len(terms) > 1:
            terms = [a + b for a, b in zip(terms[::2], terms[1::2])] + (
                [terms[-1]] if len(terms) % 2 else []
            )
        return terms[0]

    for h in range(halves):
        d = [coef_rows(dsl, h, m) for m in range(modes)]
        c = [coef_rows(csl, h, m) for m in range(modes)]

        def step(b, state):
            for u in range(UNROLL):
                t = b * UNROLL + u
                x = xs[time_rows(h, t), :]
                keep = jnp.broadcast_to(keepb[pl.ds(t, 1), :], x.shape)
                state = [(keep * s) * dm + x for s, dm in zip(state, d)]
                ys[time_rows(h, t), :] = tree([cm * s for cm, s in zip(c, state)])
            return state

        state = lax.fori_loop(0, rows // UNROLL, step, [jnp.zeros((group, 128), F32)] * modes)
        ends[h] = jnp.concatenate(state, axis=0).astype(BF16)
        for i in range(1, look + 1):
            @pl.when(k + i < n_ctx)
            def _():
                end_copy(i, h).start()

    for h in range(halves):
        for i in range(1, look + 1):
            @pl.when(k >= i)
            def _():
                end_copy(i, h).wait_recv()

        @pl.when(k > 0)
        def _():
            d = [coef_rows(dsl, h, m) for m in range(modes)]
            c = [coef_rows(csl, h, m) for m in range(modes)]
            entering = endr[h].astype(F32)
            carried = [entering[m * group : (m + 1) * group] for m in range(modes)]
            powers = list(d)
            hops = 1
            while hops < rows:
                powers = [p * p for p in powers]
                hops *= 2
            decay = powers
            for i in range(2, look + 1):
                same = jnp.where(idr[i - 1] == idr[0], 1.0, 0.0)[:group]
                same = jnp.where(k >= i, same, 0.0)
                old = endr[(i - 1) * halves + h].astype(F32)
                carried = [
                    a + jnp.where(same > 0.0, p * old[m * group : (m + 1) * group], 0.0)
                    for m, (a, p) in enumerate(zip(carried, decay))
                ]
                decay = [p * q for p, q in zip(decay, powers)]
            lead = [cm * dm * s for cm, dm, s in zip(c, d, carried)]

            def step(b, lead):
                for u in range(UNROLL):
                    t = b * UNROLL + u
                    at = time_rows(h, t)
                    alive = jnp.broadcast_to(aliveb[pl.ds(t, 1), :], (group, 128))
                    ys[at, :] = ys[at, :] + alive * tree(lead)
                    lead = [p * dm for p, dm in zip(lead, d)]
                return lead

            lax.fori_loop(0, rows // UNROLL, step, lead)

        for j in range(h * group, (h + 1) * group):
            at = slice(j * 128, (j + 1) * 128)
            slab = slice(j * rows, (j + 1) * rows)
            out[:, at] = (first[:, at].astype(F32) + xs[slab, :] * ys[slab, :]).astype(BF16)

    for i in range(1, n_chan):
        sum_copy(part1, sums1, p1_s, p1_r, i).wait_send()
        sum_copy(part2, sums2, p2_s, p2_r, i).wait_send()

    @pl.when(k + 1 < n_ctx)
    def _():
        inv_copy.wait_send()
        for q in range(chunks):
            halo_copy(q).wait_send()

    for i in range(1, look + 1):
        @pl.when(k + i < n_ctx)
        def _():
            id_copy(i).wait_send()
            for h in range(halves):
                end_copy(i, h).wait_send()


def per_device(stream, seg_ids, mr_gain, mr_filter, li_gain, decay_rates, residues):
    rows, channels = stream.shape
    modes = decay_rates.shape[1]
    n_ctx, n_chan = lax.axis_size("ctx"), lax.axis_size("chan")
    assert rows == mr_filter.shape[1]
    longest = rows * n_ctx // 4
    look = max(1, min(n_ctx - 1, -(-(longest - 1) // rows)))
    tiles = channels // 128
    group = min(8, tiles)
    halves = tiles // group
    chunks = channels // min(256, channels)
    vmem = pl.BlockSpec(memory_space=pltpu.VMEM)
    dma = pltpu.SemaphoreType.DMA
    others = max(1, n_chan - 1)
    small = (8, 128)
    tables = [jnp.asarray(t) for t in dft_tables(rows)]
    operands = (
        stream, seg_ids.reshape(1, rows), mr_gain.reshape(1, channels), mr_filter,
        li_gain.reshape(1, channels), decay_rates.T, residues.T, *tables,
    )
    return pl.pallas_call(
        partial(kernel, n_ctx, n_chan, look, channels),
        out_shape=jax.ShapeDtypeStruct((rows, channels), BF16),
        in_specs=[pl.BlockSpec(memory_space=pltpu.HBM)] * len(operands),
        out_specs=vmem,
        scratch_shapes=[pltpu.VMEM(x.shape, x.dtype) for x in operands]
        + [
            dma((len(operands),)),
            pltpu.VMEM((rows, channels), BF16),
            pltpu.VMEM((2 * rows, channels), BF16),
            pltpu.VMEM((2 * rows, channels), F32),
            pltpu.VMEM((rows, channels), BF16),
            pltpu.VMEM((tiles * rows, 128), F32),
            pltpu.VMEM((tiles * rows, 128), F32),
            pltpu.VMEM((tiles * modes, 128), F32),
            pltpu.VMEM((tiles * modes, 128), F32),
            pltpu.VMEM((rows, 128), F32),
            pltpu.VMEM((rows, 128), F32),
            pltpu.VMEM(small, F32),
            pltpu.VMEM(small, F32),
            pltpu.VMEM((others,) + small, F32),
            pltpu.VMEM((others,) + small, F32),
            pltpu.VMEM(small, F32),
            pltpu.VMEM(small, F32),
            pltpu.VMEM(small, F32),
            pltpu.VMEM((look,) + small, F32),
            pltpu.VMEM((halves, modes * group, 128), BF16),
            pltpu.VMEM((look * halves, modes * group, 128), BF16),
            dma((chunks,)), dma((chunks,)),
            dma((others,)), dma((others,)),
            dma((others,)), dma((others,)),
            dma, dma,
            dma((look,)), dma((look,)),
            dma((look * halves,)), dma((look * halves,)),
        ],
        compiler_params=pltpu.CompilerParams(
            collective_id=0, has_side_effects=True, vmem_limit_bytes=62 * 2**20
        ),
    )(*operands)


def solution(mesh):
    placed = (
        P("ctx", "chan"),
        P("ctx"),
        P("chan"),
        P("chan", None),
        P("chan"),
        P("chan", None),
        P("chan", None),
    )
    return jax.shard_map(
        per_device, mesh=mesh, in_specs=placed, out_specs=P("ctx", "chan"), check_vma=False
    )
```

```python
from functools import partial

import jax
import jax.numpy as jnp
import numpy as np
from jax import lax
from jax.experimental import pallas as pl
from jax.experimental.pallas import tpu as pltpu
from jax.sharding import PartitionSpec as P

EPSILON = 1e-06
MESH = pl.DeviceIdType.MESH
F32 = jnp.float32
BF16 = jnp.bfloat16
UNROLL = 4
PAD = 8


def split_table(table):
    high = table.astype(BF16)
    low = (table - high.astype(np.float64)).astype(BF16)
    return high, low


def dft_tables(rows):
    size = 2 * rows
    k = np.arange(rows)[:, None] + 0.5
    n = np.arange(size)[None, :]
    angle = 2.0 * np.pi * k * n / size
    forward = np.concatenate([np.cos(angle), -np.sin(angle)])
    inverse = (2.0 / size) * forward[:, rows:].T
    return split_table(forward) + split_table(inverse)


def split(x):
    high = x.astype(BF16)
    return high, (x - high.astype(F32)).astype(BF16)


def mm(a, b):
    return jnp.dot(a, b, preferred_element_type=F32)


def mm_nt(a, b):
    return lax.dot_general(a, b, (((1,), (1,)), ((), ())), preferred_element_type=F32)


def kernel(
    n_ctx, n_chan, look, width,
    *refs,
):
    sources, out, held, load_sem = refs[:11], refs[11], refs[12:23], refs[23]
    (
        halo, ext, spec, first, xs, ys, dsl, csl, keepb, aliveb,
        part1, part2, sums1, sums2, invs, invr, idb, idr, ends, endr,
        halo_s, halo_r, p1_s, p1_r, p2_s, p2_r, inv_s, inv_r, id_s, id_r, end_s, end_r,
    ) = refs[24:]
    stream, seg, gain1, taps, gain2, rates, residues, fh, fl, gh, gl = held
    loads = [
        pltpu.make_async_copy(source, target, load_sem.at[i])
        for i, (source, target) in enumerate(zip(sources, held))
    ]
    for i in (0, 1, 7, 8, 3, 5, 6, 2, 9, 10, 4):
        loads[i].start()
    rows, channels = stream.shape
    modes = rates.shape[0]
    chunk = min(256, channels)
    chunks = channels // chunk
    tiles = channels // 128
    group = min(8, tiles)
    halves = tiles // group
    pitch = rows + PAD
    k = lax.axis_index("ctx")
    z = lax.axis_index("chan")

    barrier = pltpu.get_barrier_semaphore()

    def peer(r):
        return {"chan": lax.rem(z + r, n_chan)}

    for r in range(1, n_chan):
        pl.semaphore_signal(barrier, inc=1, device_id=peer(r), device_id_type=MESH)
    for i in range(1, look + 1):
        @pl.when(k + i < n_ctx)
        def _():
            pl.semaphore_signal(barrier, inc=1, device_id={"ctx": k + i}, device_id_type=MESH)

        @pl.when(k >= i)
        def _():
            pl.semaphore_signal(barrier, inc=1, device_id={"ctx": k - i}, device_id_type=MESH)

    eye = lax.broadcasted_iota(jnp.int32, (rows, rows), 0) == lax.broadcasted_iota(
        jnp.int32, (rows, rows), 1
    )

    def to_col(row):
        return jnp.sum(jnp.where(eye, row, 0.0), axis=1, keepdims=True)

    def to_row(col):
        return jnp.sum(jnp.where(eye, col, 0.0), axis=0, keepdims=True)

    loads[0].wait()
    loads[1].wait()

    def square_step(j, acc):
        x = stream[:, pl.ds(pl.multiple_of(j * 128, 128), 128)].astype(F32)
        return acc + x * x

    acc = lax.fori_loop(0, tiles, square_step, jnp.zeros((rows, 128), F32), unroll=True)
    row = to_row(jnp.sum(acc, axis=1, keepdims=True))
    part1[...] = jnp.broadcast_to(row, part1.shape)
    segf = seg[...].astype(F32)
    lanes = lax.broadcasted_iota(jnp.int32, (1, rows), 1)
    last = jnp.sum(jnp.where(lanes == rows - 1, segf, 0.0), axis=1, keepdims=True)
    idb[...] = jnp.broadcast_to(last, idb.shape)

    peers = n_chan - 1 + jnp.minimum(k, look) + jnp.minimum(n_ctx - 1 - k, look)
    pl.semaphore_wait(barrier, peers)

    def copy(src, dst, s, r, where):
        return pltpu.make_async_remote_copy(
            src_ref=src, dst_ref=dst, send_sem=s, recv_sem=r, device_id=where, device_id_type=MESH
        )

    def sum_copy(part, sums, s, r, i):
        return copy(part, sums.at[i - 1], s.at[i - 1], r.at[i - 1], peer(i))

    def halo_copy(q):
        cols = pl.ds(pl.multiple_of(q * chunk, chunk), chunk)
        return copy(
            sources[0].at[:, cols], halo.at[:, cols], halo_s.at[q], halo_r.at[q], {"ctx": k + 1}
        )

    def id_copy(i):
        return copy(idb, idr.at[i - 1], id_s.at[i - 1], id_r.at[i - 1], {"ctx": k + i})

    def end_copy(i, h):
        e = (i - 1) * halves + h
        return copy(ends.at[h], endr.at[e], end_s.at[e], end_r.at[e], {"ctx": k + i})

    inv_copy = copy(invs, invr, inv_s, inv_r, {"ctx": k + 1})

    for i in range(1, n_chan):
        sum_copy(part1, sums1, p1_s, p1_r, i).start()

    @pl.when(k + 1 < n_ctx)
    def _():
        for q in range(chunks):
            halo_copy(q).start()

    for i in range(1, look + 1):
        @pl.when(k + i < n_ctx)
        def _():
            id_copy(i).start()

    for i in (7, 8, 3):
        loads[i].wait()

    def spectrum_step(q, c):
        at = pl.ds(pl.multiple_of(q * chunk, chunk), chunk)
        h = taps[at, :]
        spec[:, at] = mm_nt(fh[:, :rows], h) + mm_nt(fl[:, :rows], h)
        return c

    lax.fori_loop(0, chunks, spectrum_step, 0)

    for i in (5, 6, 2, 9, 10, 4):
        loads[i].wait()

    for j in range(tiles):
        at = slice(j * 128, (j + 1) * 128)
        rate = rates[:, at]
        dsl[j * modes : (j + 1) * modes, :] = jnp.exp(-rate)
        doubled = 2.0 * rate
        small = doubled * (1.0 - doubled * (0.5 - doubled * (1.0 / 6.0 - doubled * (1.0 / 24.0 - doubled * (1.0 / 120.0)))))
        gap = jnp.where(doubled < 0.05, small, 1.0 - jnp.exp(-doubled))
        csl[j * modes : (j + 1) * modes, :] = residues[:, at] * jnp.sqrt(gap)
    seg_col = to_col(segf)
    before = lax.broadcasted_iota(jnp.int32, (rows, rows), 0) - 1 == lax.broadcasted_iota(
        jnp.int32, (rows, rows), 1
    )
    prev_col = jnp.sum(jnp.where(before, segf, 0.0), axis=1, keepdims=True)
    keepb[...] = jnp.broadcast_to(jnp.where(seg_col == prev_col, 1.0, 0.0), keepb.shape)

    for i in range(1, n_chan):
        sum_copy(part1, sums1, p1_s, p1_r, i).wait_recv()
    total = part1[...]
    for i in range(1, n_chan):
        total = total + sums1[i - 1]
    full = channels * n_chan
    inverse = lax.rsqrt(total / full + EPSILON)
    invs[...] = inverse

    @pl.when(k + 1 < n_ctx)
    def _():
        inv_copy.start()

    inv_col = to_col(inverse[0:1, :])

    def norm_step(q, c):
        at = pl.ds(pl.multiple_of(q * chunk, chunk), chunk)
        ext[rows:, at] = (stream[:, at].astype(F32) * inv_col * gain1[:, at]).astype(BF16)
        return c

    lax.fori_loop(0, chunks, norm_step, 0)

    @pl.when(k > 0)
    def _():
        inv_copy.wait_recv()

    @pl.when(k == 0)
    def _():
        halo[...] = jnp.zeros_like(halo)
        invr[...] = jnp.zeros_like(invr)

    halo_col = to_col(invr[0:1, :])

    def conv_step(q, acc):
        @pl.when(k > 0)
        def _():
            halo_copy(q).wait_recv()

        at = pl.ds(pl.multiple_of(q * chunk, chunk), chunk)
        ext[:rows, at] = (halo[:, at].astype(F32) * halo_col * gain1[:, at]).astype(BF16)
        x = ext[:, at]
        freq = mm(fh[...], x) + mm(fl[...], x)
        h = spec[:, at]
        xr, xi, hr, hi = freq[:rows], freq[rows:], h[:rows], h[rows:]
        prod = jnp.concatenate([xr * hr - xi * hi, xr * hi + xi * hr], axis=0)
        ph, plow = split(prod)
        mixed = mm(gh[...], ph) + mm(gh[...], plow) + mm(gl[...], ph)
        one = stream[:, at].astype(F32) + x[rows:].astype(F32) * mixed
        one = one.astype(BF16)
        first[:, at] = one
        one = one.astype(F32)
        sq = one * one
        for s in range(chunk // 128):
            acc = acc + sq[:, s * 128 : (s + 1) * 128]
        return acc

    acc = lax.fori_loop(0, chunks, conv_step, jnp.zeros((rows, 128), F32))
    row = to_row(jnp.sum(acc, axis=1, keepdims=True))
    part2[...] = jnp.broadcast_to(row, part2.shape)
    for i in range(1, n_chan):
        sum_copy(part2, sums2, p2_s, p2_r, i).start()
    for i in range(1, look + 1):
        @pl.when(k >= i)
        def _():
            id_copy(i).wait_recv()

    @pl.when(k > 0)
    def _():
        q = idr[0]
        aliveb[...] = jnp.where(seg_col == q[0:1, :], 1.0, 0.0)

    for i in range(1, n_chan):
        sum_copy(part2, sums2, p2_s, p2_r, i).wait_recv()
    total = part2[...]
    for i in range(1, n_chan):
        total = total + sums2[i - 1]
    inv2_col = to_col(lax.rsqrt(total / full + EPSILON)[0:1, :])

    for j in range(tiles):
        at = slice(j * 128, (j + 1) * 128)
        xs[j * pitch : j * pitch + rows, :] = first[:, at].astype(F32) * inv2_col * gain2[:, at]

    def coef_rows(ref, h, m):
        return ref[pl.ds(h * group * modes + m, group, stride=modes), :]

    def time_rows(h, t):
        return pl.ds(h * group * pitch + t, group, stride=pitch)

    def tree(terms):
        while len(terms) > 1:
            terms = [a + b for a, b in zip(terms[::2], terms[1::2])] + (
                [terms[-1]] if len(terms) % 2 else []
            )
        return terms[0]

    for h in range(halves):
        d = [coef_rows(dsl, h, m) for m in range(modes)]
        c = [coef_rows(csl, h, m) for m in range(modes)]

        def step(b, state):
            for u in range(UNROLL):
                t = b * UNROLL + u
                x = xs[time_rows(h, t), :]
                keep = jnp.broadcast_to(keepb[pl.ds(t, 1), :], x.shape)
                state = [(keep * s) * dm + x for s, dm in zip(state, d)]
                ys[time_rows(h, t), :] = tree([cm * s for cm, s in zip(c, state)])
            return state

        state = lax.fori_loop(0, rows // UNROLL, step, [jnp.zeros((group, 128), F32)] * modes)
        ends[h] = jnp.concatenate(state, axis=0).astype(BF16)
        for i in range(1, look + 1):
            @pl.when(k + i < n_ctx)
            def _():
                end_copy(i, h).start()

    for h in range(halves):
        for i in range(1, look + 1):
            @pl.when(k >= i)
            def _():
                end_copy(i, h).wait_recv()

        @pl.when(k > 0)
        def _():
            d = [coef_rows(dsl, h, m) for m in range(modes)]
            c = [coef_rows(csl, h, m) for m in range(modes)]
            entering = endr[h].astype(F32)
            carried = [entering[m * group : (m + 1) * group] for m in range(modes)]
            powers = list(d)
            hops = 1
            while hops < rows:
                powers = [p * p for p in powers]
                hops *= 2
            decay = powers
            for i in range(2, look + 1):
                same = jnp.where(idr[i - 1] == idr[0], 1.0, 0.0)[:group]
                same = jnp.where(k >= i, same, 0.0)
                old = endr[(i - 1) * halves + h].astype(F32)
                carried = [
                    a + jnp.where(same > 0.0, p * old[m * group : (m + 1) * group], 0.0)
                    for m, (a, p) in enumerate(zip(carried, decay))
                ]
                decay = [p * q for p, q in zip(decay, powers)]
            lead = [cm * dm * s for cm, dm, s in zip(c, d, carried)]

            def step(b, lead):
                for u in range(UNROLL):
                    t = b * UNROLL + u
                    at = time_rows(h, t)
                    alive = jnp.broadcast_to(aliveb[pl.ds(t, 1), :], (group, 128))
                    ys[at, :] = ys[at, :] + alive * tree(lead)
                    lead = [p * dm for p, dm in zip(lead, d)]
                return lead

            lax.fori_loop(0, rows // UNROLL, step, lead)

        for j in range(h * group, (h + 1) * group):
            at = slice(j * 128, (j + 1) * 128)
            slab = slice(j * pitch, j * pitch + rows)
            out[:, at] = (first[:, at].astype(F32) + xs[slab, :] * ys[slab, :]).astype(BF16)

    for i in range(1, n_chan):
        sum_copy(part1, sums1, p1_s, p1_r, i).wait_send()
        sum_copy(part2, sums2, p2_s, p2_r, i).wait_send()

    @pl.when(k + 1 < n_ctx)
    def _():
        inv_copy.wait_send()
        for q in range(chunks):
            halo_copy(q).wait_send()

    for i in range(1, look + 1):
        @pl.when(k + i < n_ctx)
        def _():
            id_copy(i).wait_send()
            for h in range(halves):
                end_copy(i, h).wait_send()


def per_device(stream, seg_ids, mr_gain, mr_filter, li_gain, decay_rates, residues):
    rows, channels = stream.shape
    modes = decay_rates.shape[1]
    n_ctx, n_chan = lax.axis_size("ctx"), lax.axis_size("chan")
    assert rows == mr_filter.shape[1]
    longest = rows * n_ctx // 4
    look = max(1, min(n_ctx - 1, -(-(longest - 1) // rows)))
    tiles = channels // 128
    group = min(8, tiles)
    halves = tiles // group
    chunks = channels // min(256, channels)
    vmem = pl.BlockSpec(memory_space=pltpu.VMEM)
    dma = pltpu.SemaphoreType.DMA
    others = max(1, n_chan - 1)
    small = (8, 128)
    tables = [jnp.asarray(t) for t in dft_tables(rows)]
    operands = (
        stream, seg_ids.reshape(1, rows), mr_gain.reshape(1, channels), mr_filter,
        li_gain.reshape(1, channels), decay_rates.T, residues.T, *tables,
    )
    return pl.pallas_call(
        partial(kernel, n_ctx, n_chan, look, channels),
        out_shape=jax.ShapeDtypeStruct((rows, channels), BF16),
        in_specs=[pl.BlockSpec(memory_space=pltpu.HBM)] * len(operands),
        out_specs=vmem,
        scratch_shapes=[pltpu.VMEM(x.shape, x.dtype) for x in operands]
        + [
            dma((len(operands),)),
            pltpu.VMEM((rows, channels), BF16),
            pltpu.VMEM((2 * rows, channels), BF16),
            pltpu.VMEM((2 * rows, channels), F32),
            pltpu.VMEM((rows, channels), BF16),
            pltpu.VMEM((tiles * (rows + PAD), 128), F32),
            pltpu.VMEM((tiles * (rows + PAD), 128), F32),
            pltpu.VMEM((tiles * modes, 128), F32),
            pltpu.VMEM((tiles * modes, 128), F32),
            pltpu.VMEM((rows, 128), F32),
            pltpu.VMEM((rows, 128), F32),
            pltpu.VMEM(small, F32),
            pltpu.VMEM(small, F32),
            pltpu.VMEM((others,) + small, F32),
            pltpu.VMEM((others,) + small, F32),
            pltpu.VMEM(small, F32),
            pltpu.VMEM(small, F32),
            pltpu.VMEM(small, F32),
            pltpu.VMEM((look,) + small, F32),
            pltpu.VMEM((halves, modes * group, 128), BF16),
            pltpu.VMEM((look * halves, modes * group, 128), BF16),
            dma((chunks,)), dma((chunks,)),
            dma((others,)), dma((others,)),
            dma((others,)), dma((others,)),
            dma, dma,
            dma((look,)), dma((look,)),
            dma((look * halves,)), dma((look * halves,)),
        ],
        compiler_params=pltpu.CompilerParams(
            collective_id=0, has_side_effects=True, vmem_limit_bytes=62 * 2**20
        ),
    )(*operands)


def solution(mesh):
    placed = (
        P("ctx", "chan"),
        P("ctx"),
        P("chan"),
        P("chan", None),
        P("chan"),
        P("chan", None),
        P("chan", None),
    )
    return jax.shard_map(
        per_device, mesh=mesh, in_specs=placed, out_specs=P("ctx", "chan"), check_vma=False
    )
```

```python
from functools import partial

import jax
import jax.numpy as jnp
import numpy as np
from jax import lax
from jax.experimental import pallas as pl
from jax.experimental.pallas import tpu as pltpu
from jax.sharding import PartitionSpec as P

EPSILON = 1e-06
MESH = pl.DeviceIdType.MESH
F32 = jnp.float32
BF16 = jnp.bfloat16
UNROLL = 8
PAD = 8


def split_table(table):
    high = table.astype(BF16)
    low = (table - high.astype(np.float64)).astype(BF16)
    return high, low


def dft_tables(rows):
    size = 2 * rows
    k = np.arange(rows)[:, None] + 0.5
    n = np.arange(size)[None, :]
    angle = 2.0 * np.pi * k * n / size
    forward = np.concatenate([np.cos(angle), -np.sin(angle)])
    inverse = (2.0 / size) * forward[:, rows:].T
    return split_table(forward) + split_table(inverse)


def split(x):
    high = x.astype(BF16)
    return high, (x - high.astype(F32)).astype(BF16)


def mm(a, b):
    return jnp.dot(a, b, preferred_element_type=F32)


def mm_nt(a, b):
    return lax.dot_general(a, b, (((1,), (1,)), ((), ())), preferred_element_type=F32)


def kernel(
    n_ctx, n_chan, look, width,
    *refs,
):
    sources, out, held, load_sem = refs[:11], refs[11], refs[12:23], refs[23]
    (
        halo, ext, spec, first, xs, ys, dsl, csl, keepb, aliveb,
        part1, part2, sums1, sums2, invs, invr, idb, idr, ends, endr,
        halo_s, halo_r, p1_s, p1_r, p2_s, p2_r, inv_s, inv_r, id_s, id_r, end_s, end_r,
    ) = refs[24:]
    stream, seg, gain1, taps, gain2, rates, residues, fh, fl, gh, gl = held
    loads = [
        pltpu.make_async_copy(source, target, load_sem.at[i])
        for i, (source, target) in enumerate(zip(sources, held))
    ]
    for i in (0, 1, 7, 8, 3, 5, 6, 2, 9, 10, 4):
        loads[i].start()
    rows, channels = stream.shape
    modes = rates.shape[0]
    chunk = min(256, channels)
    chunks = channels // chunk
    tiles = channels // 128
    group = min(8, tiles)
    halves = tiles // group
    pitch = rows + PAD
    k = lax.axis_index("ctx")
    z = lax.axis_index("chan")

    barrier = pltpu.get_barrier_semaphore()

    def peer(r):
        return {"chan": lax.rem(z + r, n_chan)}

    for r in range(1, n_chan):
        pl.semaphore_signal(barrier, inc=1, device_id=peer(r), device_id_type=MESH)
    for i in range(1, look + 1):
        @pl.when(k + i < n_ctx)
        def _():
            pl.semaphore_signal(barrier, inc=1, device_id={"ctx": k + i}, device_id_type=MESH)

        @pl.when(k >= i)
        def _():
            pl.semaphore_signal(barrier, inc=1, device_id={"ctx": k - i}, device_id_type=MESH)

    eye = lax.broadcasted_iota(jnp.int32, (rows, rows), 0) == lax.broadcasted_iota(
        jnp.int32, (rows, rows), 1
    )

    def to_col(row):
        return jnp.sum(jnp.where(eye, row, 0.0), axis=1, keepdims=True)

    def to_row(col):
        return jnp.sum(jnp.where(eye, col, 0.0), axis=0, keepdims=True)

    loads[0].wait()
    loads[1].wait()

    def square_step(j, acc):
        x = stream[:, pl.ds(pl.multiple_of(j * 128, 128), 128)].astype(F32)
        return acc + x * x

    acc = lax.fori_loop(0, tiles, square_step, jnp.zeros((rows, 128), F32), unroll=True)
    row = to_row(jnp.sum(acc, axis=1, keepdims=True))
    part1[...] = jnp.broadcast_to(row, part1.shape)
    segf = seg[...].astype(F32)
    lanes = lax.broadcasted_iota(jnp.int32, (1, rows), 1)
    last = jnp.sum(jnp.where(lanes == rows - 1, segf, 0.0), axis=1, keepdims=True)
    idb[...] = jnp.broadcast_to(last, idb.shape)

    peers = n_chan - 1 + jnp.minimum(k, look) + jnp.minimum(n_ctx - 1 - k, look)
    pl.semaphore_wait(barrier, peers)

    def copy(src, dst, s, r, where):
        return pltpu.make_async_remote_copy(
            src_ref=src, dst_ref=dst, send_sem=s, recv_sem=r, device_id=where, device_id_type=MESH
        )

    def sum_copy(part, sums, s, r, i):
        return copy(part, sums.at[i - 1], s.at[i - 1], r.at[i - 1], peer(i))

    def halo_copy(q):
        cols = pl.ds(pl.multiple_of(q * chunk, chunk), chunk)
        return copy(
            sources[0].at[:, cols], halo.at[:, cols], halo_s.at[q], halo_r.at[q], {"ctx": k + 1}
        )

    def id_copy(i):
        return copy(idb, idr.at[i - 1], id_s.at[i - 1], id_r.at[i - 1], {"ctx": k + i})

    def end_copy(i, h):
        e = (i - 1) * halves + h
        return copy(ends.at[h], endr.at[e], end_s.at[e], end_r.at[e], {"ctx": k + i})

    inv_copy = copy(invs, invr, inv_s, inv_r, {"ctx": k + 1})

    for i in range(1, n_chan):
        sum_copy(part1, sums1, p1_s, p1_r, i).start()

    @pl.when(k + 1 < n_ctx)
    def _():
        for q in range(chunks):
            halo_copy(q).start()

    for i in range(1, look + 1):
        @pl.when(k + i < n_ctx)
        def _():
            id_copy(i).start()

    for i in (7, 8, 3):
        loads[i].wait()

    def spectrum_step(q, c):
        at = pl.ds(pl.multiple_of(q * chunk, chunk), chunk)
        h = taps[at, :]
        spec[:, at] = mm_nt(fh[:, :rows], h) + mm_nt(fl[:, :rows], h)
        return c

    lax.fori_loop(0, chunks, spectrum_step, 0)

    for i in (5, 6, 2, 9, 10, 4):
        loads[i].wait()

    for j in range(tiles):
        at = slice(j * 128, (j + 1) * 128)
        rate = rates[:, at]
        dsl[j * modes : (j + 1) * modes, :] = jnp.exp(-rate)
        doubled = 2.0 * rate
        small = doubled * (1.0 - doubled * (0.5 - doubled * (1.0 / 6.0 - doubled * (1.0 / 24.0 - doubled * (1.0 / 120.0)))))
        gap = jnp.where(doubled < 0.05, small, 1.0 - jnp.exp(-doubled))
        csl[j * modes : (j + 1) * modes, :] = residues[:, at] * jnp.sqrt(gap)
    seg_col = to_col(segf)
    before = lax.broadcasted_iota(jnp.int32, (rows, rows), 0) - 1 == lax.broadcasted_iota(
        jnp.int32, (rows, rows), 1
    )
    prev_col = jnp.sum(jnp.where(before, segf, 0.0), axis=1, keepdims=True)
    keepb[...] = jnp.broadcast_to(jnp.where(seg_col == prev_col, 1.0, 0.0), keepb.shape)

    for i in range(1, n_chan):
        sum_copy(part1, sums1, p1_s, p1_r, i).wait_recv()
    total = part1[...]
    for i in range(1, n_chan):
        total = total + sums1[i - 1]
    full = channels * n_chan
    inverse = lax.rsqrt(total / full + EPSILON)
    invs[...] = inverse

    @pl.when(k + 1 < n_ctx)
    def _():
        inv_copy.start()

    inv_col = to_col(inverse[0:1, :])

    def norm_step(q, c):
        at = pl.ds(pl.multiple_of(q * chunk, chunk), chunk)
        ext[rows:, at] = (stream[:, at].astype(F32) * inv_col * gain1[:, at]).astype(BF16)
        return c

    lax.fori_loop(0, chunks, norm_step, 0)

    @pl.when(k > 0)
    def _():
        inv_copy.wait_recv()

    @pl.when(k == 0)
    def _():
        halo[...] = jnp.zeros_like(halo)
        invr[...] = jnp.zeros_like(invr)

    halo_col = to_col(invr[0:1, :])

    def conv_step(q, acc):
        @pl.when(k > 0)
        def _():
            halo_copy(q).wait_recv()

        at = pl.ds(pl.multiple_of(q * chunk, chunk), chunk)
        ext[:rows, at] = (halo[:, at].astype(F32) * halo_col * gain1[:, at]).astype(BF16)
        x = ext[:, at]
        freq = mm(fh[...], x) + mm(fl[...], x)
        h = spec[:, at]
        xr, xi, hr, hi = freq[:rows], freq[rows:], h[:rows], h[rows:]
        prod = jnp.concatenate([xr * hr - xi * hi, xr * hi + xi * hr], axis=0)
        ph, plow = split(prod)
        mixed = mm(gh[...], ph) + mm(gh[...], plow) + mm(gl[...], ph)
        one = stream[:, at].astype(F32) + x[rows:].astype(F32) * mixed
        one = one.astype(BF16)
        first[:, at] = one
        one = one.astype(F32)
        sq = one * one
        for s in range(chunk // 128):
            acc = acc + sq[:, s * 128 : (s + 1) * 128]
        return acc

    acc = lax.fori_loop(0, chunks, conv_step, jnp.zeros((rows, 128), F32))
    row = to_row(jnp.sum(acc, axis=1, keepdims=True))
    part2[...] = jnp.broadcast_to(row, part2.shape)
    for i in range(1, n_chan):
        sum_copy(part2, sums2, p2_s, p2_r, i).start()
    for i in range(1, look + 1):
        @pl.when(k >= i)
        def _():
            id_copy(i).wait_recv()

    @pl.when(k > 0)
    def _():
        q = idr[0]
        aliveb[...] = jnp.where(seg_col == q[0:1, :], 1.0, 0.0)

    for i in range(1, n_chan):
        sum_copy(part2, sums2, p2_s, p2_r, i).wait_recv()
    total = part2[...]
    for i in range(1, n_chan):
        total = total + sums2[i - 1]
    inv2_col = to_col(lax.rsqrt(total / full + EPSILON)[0:1, :])

    for j in range(tiles):
        at = slice(j * 128, (j + 1) * 128)
        xs[j * pitch : j * pitch + rows, :] = first[:, at].astype(F32) * inv2_col * gain2[:, at]

    def coef_rows(ref, h, m):
        return ref[pl.ds(h * group * modes + m, group, stride=modes), :]

    def time_rows(h, t):
        return pl.ds(h * group * pitch + t, group, stride=pitch)

    def tree(terms):
        while len(terms) > 1:
            terms = [a + b for a, b in zip(terms[::2], terms[1::2])] + (
                [terms[-1]] if len(terms) % 2 else []
            )
        return terms[0]

    for h in range(halves):
        d = [coef_rows(dsl, h, m) for m in range(modes)]
        c = [coef_rows(csl, h, m) for m in range(modes)]

        def step(b, state):
            for u in range(UNROLL):
                t = b * UNROLL + u
                x = xs[time_rows(h, t), :]
                keep = jnp.broadcast_to(keepb[pl.ds(t, 1), :], x.shape)
                state = [(keep * s) * dm + x for s, dm in zip(state, d)]
                ys[time_rows(h, t), :] = tree([cm * s for cm, s in zip(c, state)])
            return state

        state = lax.fori_loop(0, rows // UNROLL, step, [jnp.zeros((group, 128), F32)] * modes)
        ends[h] = jnp.concatenate(state, axis=0).astype(BF16)
        for i in range(1, look + 1):
            @pl.when(k + i < n_ctx)
            def _():
                end_copy(i, h).start()

    for h in range(halves):
        for i in range(1, look + 1):
            @pl.when(k >= i)
            def _():
                end_copy(i, h).wait_recv()

        @pl.when(k > 0)
        def _():
            d = [coef_rows(dsl, h, m) for m in range(modes)]
            c = [coef_rows(csl, h, m) for m in range(modes)]
            entering = endr[h].astype(F32)
            carried = [entering[m * group : (m + 1) * group] for m in range(modes)]
            powers = list(d)
            hops = 1
            while hops < rows:
                powers = [p * p for p in powers]
                hops *= 2
            decay = powers
            for i in range(2, look + 1):
                same = jnp.where(idr[i - 1] == idr[0], 1.0, 0.0)[:group]
                same = jnp.where(k >= i, same, 0.0)
                old = endr[(i - 1) * halves + h].astype(F32)
                carried = [
                    a + jnp.where(same > 0.0, p * old[m * group : (m + 1) * group], 0.0)
                    for m, (a, p) in enumerate(zip(carried, decay))
                ]
                decay = [p * q for p, q in zip(decay, powers)]
            lead = [cm * dm * s for cm, dm, s in zip(c, d, carried)]

            def step(b, lead):
                for u in range(UNROLL):
                    t = b * UNROLL + u
                    at = time_rows(h, t)
                    alive = jnp.broadcast_to(aliveb[pl.ds(t, 1), :], (group, 128))
                    ys[at, :] = ys[at, :] + alive * tree(lead)
                    lead = [p * dm for p, dm in zip(lead, d)]
                return lead

            lax.fori_loop(0, rows // UNROLL, step, lead)

        for j in range(h * group, (h + 1) * group):
            at = slice(j * 128, (j + 1) * 128)
            slab = slice(j * pitch, j * pitch + rows)
            out[:, at] = (first[:, at].astype(F32) + xs[slab, :] * ys[slab, :]).astype(BF16)

    for i in range(1, n_chan):
        sum_copy(part1, sums1, p1_s, p1_r, i).wait_send()
        sum_copy(part2, sums2, p2_s, p2_r, i).wait_send()

    @pl.when(k + 1 < n_ctx)
    def _():
        inv_copy.wait_send()
        for q in range(chunks):
            halo_copy(q).wait_send()

    for i in range(1, look + 1):
        @pl.when(k + i < n_ctx)
        def _():
            id_copy(i).wait_send()
            for h in range(halves):
                end_copy(i, h).wait_send()


def per_device(stream, seg_ids, mr_gain, mr_filter, li_gain, decay_rates, residues):
    rows, channels = stream.shape
    modes = decay_rates.shape[1]
    n_ctx, n_chan = lax.axis_size("ctx"), lax.axis_size("chan")
    assert rows == mr_filter.shape[1]
    longest = rows * n_ctx // 4
    look = max(1, min(n_ctx - 1, -(-(longest - 1) // rows)))
    tiles = channels // 128
    group = min(8, tiles)
    halves = tiles // group
    chunks = channels // min(256, channels)
    vmem = pl.BlockSpec(memory_space=pltpu.VMEM)
    dma = pltpu.SemaphoreType.DMA
    others = max(1, n_chan - 1)
    small = (8, 128)
    tables = [jnp.asarray(t) for t in dft_tables(rows)]
    operands = (
        stream, seg_ids.reshape(1, rows), mr_gain.reshape(1, channels), mr_filter,
        li_gain.reshape(1, channels), decay_rates.T, residues.T, *tables,
    )
    return pl.pallas_call(
        partial(kernel, n_ctx, n_chan, look, channels),
        out_shape=pltpu.VMEM((rows, channels), BF16),
        in_specs=[pl.BlockSpec(memory_space=pltpu.HBM)] * len(operands),
        out_specs=vmem,
        scratch_shapes=[pltpu.VMEM(x.shape, x.dtype) for x in operands]
        + [
            dma((len(operands),)),
            pltpu.VMEM((rows, channels), BF16),
            pltpu.VMEM((2 * rows, channels), BF16),
            pltpu.VMEM((2 * rows, channels), F32),
            pltpu.VMEM((rows, channels), BF16),
            pltpu.VMEM((tiles * (rows + PAD), 128), F32),
            pltpu.VMEM((tiles * (rows + PAD), 128), F32),
            pltpu.VMEM((tiles * modes, 128), F32),
            pltpu.VMEM((tiles * modes, 128), F32),
            pltpu.VMEM((rows, 128), F32),
            pltpu.VMEM((rows, 128), F32),
            pltpu.VMEM(small, F32),
            pltpu.VMEM(small, F32),
            pltpu.VMEM((others,) + small, F32),
            pltpu.VMEM((others,) + small, F32),
            pltpu.VMEM(small, F32),
            pltpu.VMEM(small, F32),
            pltpu.VMEM(small, F32),
            pltpu.VMEM((look,) + small, F32),
            pltpu.VMEM((halves, modes * group, 128), BF16),
            pltpu.VMEM((look * halves, modes * group, 128), BF16),
            dma((chunks,)), dma((chunks,)),
            dma((others,)), dma((others,)),
            dma((others,)), dma((others,)),
            dma, dma,
            dma((look,)), dma((look,)),
            dma((look * halves,)), dma((look * halves,)),
        ],
        compiler_params=pltpu.CompilerParams(
            collective_id=0, has_side_effects=True, vmem_limit_bytes=56 * 2**20
        ),
    )(*operands)


def solution(mesh):
    placed = (
        P("ctx", "chan"),
        P("ctx"),
        P("chan"),
        P("chan", None),
        P("chan"),
        P("chan", None),
        P("chan", None),
    )
    return jax.shard_map(
        per_device, mesh=mesh, in_specs=placed, out_specs=P("ctx", "chan"), check_vma=False
    )
```

```python
from functools import partial

import jax
import jax.numpy as jnp
import numpy as np
from jax import lax
from jax.experimental import pallas as pl
from jax.experimental.pallas import tpu as pltpu
from jax.sharding import PartitionSpec as P

EPSILON = 1e-06
MESH = pl.DeviceIdType.MESH
F32 = jnp.float32
BF16 = jnp.bfloat16
UNROLL = 8
PAD = 8


def split_table(table):
    high = table.astype(BF16)
    low = (table - high.astype(np.float64)).astype(BF16)
    return high, low


def dft_tables(rows):
    size = 2 * rows
    k = np.arange(rows)[:, None] + 0.5
    n = np.arange(size)[None, :]
    angle = 2.0 * np.pi * k * n / size
    forward = np.concatenate([np.cos(angle), -np.sin(angle)])
    inverse = (2.0 / size) * forward[:, rows:].T
    return split_table(forward) + split_table(inverse)


def split(x):
    high = x.astype(BF16)
    return high, (x - high.astype(F32)).astype(BF16)


def mm(a, b):
    return jnp.dot(a, b, preferred_element_type=F32)


def mm_nt(a, b):
    return lax.dot_general(a, b, (((1,), (1,)), ((), ())), preferred_element_type=F32)


def kernel(
    n_ctx, n_chan, look, width,
    *refs,
):
    sources, out, held, load_sem = refs[:11], refs[11], refs[12:23], refs[23]
    (
        halo, ext, spec, first, xs, ys, dsl, csl, keepb, aliveb,
        part1, part2, sums1, sums2, invs, invr, idb, idr, ends, endr,
        halo_s, halo_r, p1_s, p1_r, p2_s, p2_r, inv_s, inv_r, id_s, id_r, end_s, end_r,
    ) = refs[24:]
    stream, seg, gain1, taps, gain2, rates, residues, fh, fl, gh, gl = held
    loads = [
        pltpu.make_async_copy(source, target, load_sem.at[i])
        for i, (source, target) in enumerate(zip(sources, held))
    ]
    for i in (0, 1, 7, 8, 3, 5, 6, 2, 9, 10, 4):
        loads[i].start()
    rows, channels = stream.shape
    modes = rates.shape[0]
    chunk = min(512, channels)
    chunks = channels // chunk
    tiles = channels // 128
    group = min(8, tiles)
    halves = tiles // group
    pitch = rows + PAD
    k = lax.axis_index("ctx")
    z = lax.axis_index("chan")

    barrier = pltpu.get_barrier_semaphore()

    def peer(r):
        return {"chan": lax.rem(z + r, n_chan)}

    for r in range(1, n_chan):
        pl.semaphore_signal(barrier, inc=1, device_id=peer(r), device_id_type=MESH)
    for i in range(1, look + 1):
        @pl.when(k + i < n_ctx)
        def _():
            pl.semaphore_signal(barrier, inc=1, device_id={"ctx": k + i}, device_id_type=MESH)

        @pl.when(k >= i)
        def _():
            pl.semaphore_signal(barrier, inc=1, device_id={"ctx": k - i}, device_id_type=MESH)

    eye = lax.broadcasted_iota(jnp.int32, (rows, rows), 0) == lax.broadcasted_iota(
        jnp.int32, (rows, rows), 1
    )

    def to_col(row):
        return jnp.sum(jnp.where(eye, row, 0.0), axis=1, keepdims=True)

    def to_row(col):
        return jnp.sum(jnp.where(eye, col, 0.0), axis=0, keepdims=True)

    loads[0].wait()
    loads[1].wait()

    def square_step(j, acc):
        x = stream[:, pl.ds(pl.multiple_of(j * 128, 128), 128)].astype(F32)
        return acc + x * x

    acc = lax.fori_loop(0, tiles, square_step, jnp.zeros((rows, 128), F32), unroll=True)
    row = to_row(jnp.sum(acc, axis=1, keepdims=True))
    part1[...] = jnp.broadcast_to(row, part1.shape)
    segf = seg[...].astype(F32)
    lanes = lax.broadcasted_iota(jnp.int32, (1, rows), 1)
    last = jnp.sum(jnp.where(lanes == rows - 1, segf, 0.0), axis=1, keepdims=True)
    idb[...] = jnp.broadcast_to(last, idb.shape)

    peers = n_chan - 1 + jnp.minimum(k, look) + jnp.minimum(n_ctx - 1 - k, look)
    pl.semaphore_wait(barrier, peers)

    def copy(src, dst, s, r, where):
        return pltpu.make_async_remote_copy(
            src_ref=src, dst_ref=dst, send_sem=s, recv_sem=r, device_id=where, device_id_type=MESH
        )

    def sum_copy(part, sums, s, r, i):
        return copy(part, sums.at[i - 1], s.at[i - 1], r.at[i - 1], peer(i))

    def halo_copy(q):
        cols = pl.ds(pl.multiple_of(q * chunk, chunk), chunk)
        return copy(
            sources[0].at[:, cols], halo.at[:, cols], halo_s.at[q], halo_r.at[q], {"ctx": k + 1}
        )

    def id_copy(i):
        return copy(idb, idr.at[i - 1], id_s.at[i - 1], id_r.at[i - 1], {"ctx": k + i})

    def end_copy(i, h):
        e = (i - 1) * halves + h
        return copy(ends.at[h], endr.at[e], end_s.at[e], end_r.at[e], {"ctx": k + i})

    inv_copy = copy(invs, invr, inv_s, inv_r, {"ctx": k + 1})

    for i in range(1, n_chan):
        sum_copy(part1, sums1, p1_s, p1_r, i).start()

    @pl.when(k + 1 < n_ctx)
    def _():
        for q in range(chunks):
            halo_copy(q).start()

    for i in range(1, look + 1):
        @pl.when(k + i < n_ctx)
        def _():
            id_copy(i).start()

    for i in (7, 8, 3):
        loads[i].wait()

    def spectrum_step(q, c):
        at = pl.ds(pl.multiple_of(q * chunk, chunk), chunk)
        h = taps[at, :]
        spec[:, at] = mm_nt(fh[:, :rows], h) + mm_nt(fl[:, :rows], h)
        return c

    lax.fori_loop(0, chunks, spectrum_step, 0)

    for i in (5, 6, 2, 9, 10, 4):
        loads[i].wait()

    for j in range(tiles):
        at = slice(j * 128, (j + 1) * 128)
        rate = rates[:, at]
        dsl[j * modes : (j + 1) * modes, :] = jnp.exp(-rate)
        doubled = 2.0 * rate
        small = doubled * (1.0 - doubled * (0.5 - doubled * (1.0 / 6.0 - doubled * (1.0 / 24.0 - doubled * (1.0 / 120.0)))))
        gap = jnp.where(doubled < 0.05, small, 1.0 - jnp.exp(-doubled))
        csl[j * modes : (j + 1) * modes, :] = residues[:, at] * jnp.sqrt(gap)
    seg_col = to_col(segf)
    before = lax.broadcasted_iota(jnp.int32, (rows, rows), 0) - 1 == lax.broadcasted_iota(
        jnp.int32, (rows, rows), 1
    )
    prev_col = jnp.sum(jnp.where(before, segf, 0.0), axis=1, keepdims=True)
    keepb[...] = jnp.broadcast_to(jnp.where(seg_col == prev_col, 1.0, 0.0), keepb.shape)

    for i in range(1, n_chan):
        sum_copy(part1, sums1, p1_s, p1_r, i).wait_recv()
    total = part1[...]
    for i in range(1, n_chan):
        total = total + sums1[i - 1]
    full = channels * n_chan
    inverse = lax.rsqrt(total / full + EPSILON)
    invs[...] = inverse

    @pl.when(k + 1 < n_ctx)
    def _():
        inv_copy.start()

    inv_col = to_col(inverse[0:1, :])

    def norm_step(q, c):
        at = pl.ds(pl.multiple_of(q * chunk, chunk), chunk)
        ext[rows:, at] = (stream[:, at].astype(F32) * inv_col * gain1[:, at]).astype(BF16)
        return c

    lax.fori_loop(0, chunks, norm_step, 0)

    @pl.when(k > 0)
    def _():
        inv_copy.wait_recv()

    @pl.when(k == 0)
    def _():
        halo[...] = jnp.zeros_like(halo)
        invr[...] = jnp.zeros_like(invr)

    halo_col = to_col(invr[0:1, :])

    def conv_step(q, acc):
        @pl.when(k > 0)
        def _():
            halo_copy(q).wait_recv()

        at = pl.ds(pl.multiple_of(q * chunk, chunk), chunk)
        ext[:rows, at] = (halo[:, at].astype(F32) * halo_col * gain1[:, at]).astype(BF16)
        x = ext[:, at]
        freq = mm(fh[...], x) + mm(fl[...], x)
        h = spec[:, at]
        xr, xi, hr, hi = freq[:rows], freq[rows:], h[:rows], h[rows:]
        prod = jnp.concatenate([xr * hr - xi * hi, xr * hi + xi * hr], axis=0)
        ph, plow = split(prod)
        mixed = mm(gh[...], ph) + mm(gh[...], plow) + mm(gl[...], ph)
        one = stream[:, at].astype(F32) + x[rows:].astype(F32) * mixed
        one = one.astype(BF16)
        first[:, at] = one
        one = one.astype(F32)
        sq = one * one
        for s in range(chunk // 128):
            acc = acc + sq[:, s * 128 : (s + 1) * 128]
        return acc

    acc = lax.fori_loop(0, chunks, conv_step, jnp.zeros((rows, 128), F32))
    row = to_row(jnp.sum(acc, axis=1, keepdims=True))
    part2[...] = jnp.broadcast_to(row, part2.shape)
    for i in range(1, n_chan):
        sum_copy(part2, sums2, p2_s, p2_r, i).start()
    for i in range(1, look + 1):
        @pl.when(k >= i)
        def _():
            id_copy(i).wait_recv()

    @pl.when(k > 0)
    def _():
        q = idr[0]
        aliveb[...] = jnp.where(seg_col == q[0:1, :], 1.0, 0.0)

    for i in range(1, n_chan):
        sum_copy(part2, sums2, p2_s, p2_r, i).wait_recv()
    total = part2[...]
    for i in range(1, n_chan):
        total = total + sums2[i - 1]
    inv2_col = to_col(lax.rsqrt(total / full + EPSILON)[0:1, :])

    for j in range(tiles):
        at = slice(j * 128, (j + 1) * 128)
        xs[j * pitch : j * pitch + rows, :] = first[:, at].astype(F32) * inv2_col * gain2[:, at]

    def coef_rows(ref, h, m):
        return ref[pl.ds(h * group * modes + m, group, stride=modes), :]

    def time_rows(h, t):
        return pl.ds(h * group * pitch + t, group, stride=pitch)

    def tree(terms):
        while len(terms) > 1:
            terms = [a + b for a, b in zip(terms[::2], terms[1::2])] + (
                [terms[-1]] if len(terms) % 2 else []
            )
        return terms[0]

    for h in range(halves):
        d = [coef_rows(dsl, h, m) for m in range(modes)]
        c = [coef_rows(csl, h, m) for m in range(modes)]

        def step(b, state):
            for u in range(UNROLL):
                t = b * UNROLL + u
                x = xs[time_rows(h, t), :]
                keep = jnp.broadcast_to(keepb[pl.ds(t, 1), :], x.shape)
                state = [(keep * s) * dm + x for s, dm in zip(state, d)]
                ys[time_rows(h, t), :] = tree([cm * s for cm, s in zip(c, state)])
            return state

        state = lax.fori_loop(0, rows // UNROLL, step, [jnp.zeros((group, 128), F32)] * modes)
        ends[h] = jnp.concatenate(state, axis=0).astype(BF16)
        for i in range(1, look + 1):
            @pl.when(k + i < n_ctx)
            def _():
                end_copy(i, h).start()

    for h in range(halves):
        for i in range(1, look + 1):
            @pl.when(k >= i)
            def _():
                end_copy(i, h).wait_recv()

        @pl.when(k > 0)
        def _():
            d = [coef_rows(dsl, h, m) for m in range(modes)]
            c = [coef_rows(csl, h, m) for m in range(modes)]
            entering = endr[h].astype(F32)
            carried = [entering[m * group : (m + 1) * group] for m in range(modes)]
            powers = list(d)
            hops = 1
            while hops < rows:
                powers = [p * p for p in powers]
                hops *= 2
            decay = powers
            for i in range(2, look + 1):
                same = jnp.where(idr[i - 1] == idr[0], 1.0, 0.0)[:group]
                same = jnp.where(k >= i, same, 0.0)
                old = endr[(i - 1) * halves + h].astype(F32)
                carried = [
                    a + jnp.where(same > 0.0, p * old[m * group : (m + 1) * group], 0.0)
                    for m, (a, p) in enumerate(zip(carried, decay))
                ]
                decay = [p * q for p, q in zip(decay, powers)]
            lead = [cm * dm * s for cm, dm, s in zip(c, d, carried)]

            def step(b, lead):
                for u in range(UNROLL):
                    t = b * UNROLL + u
                    at = time_rows(h, t)
                    alive = jnp.broadcast_to(aliveb[pl.ds(t, 1), :], (group, 128))
                    ys[at, :] = ys[at, :] + alive * tree(lead)
                    lead = [p * dm for p, dm in zip(lead, d)]
                return lead

            lax.fori_loop(0, rows // UNROLL, step, lead)

        for j in range(h * group, (h + 1) * group):
            at = slice(j * 128, (j + 1) * 128)
            slab = slice(j * pitch, j * pitch + rows)
            out[:, at] = (first[:, at].astype(F32) + xs[slab, :] * ys[slab, :]).astype(BF16)

    for i in range(1, n_chan):
        sum_copy(part1, sums1, p1_s, p1_r, i).wait_send()
        sum_copy(part2, sums2, p2_s, p2_r, i).wait_send()

    @pl.when(k + 1 < n_ctx)
    def _():
        inv_copy.wait_send()
        for q in range(chunks):
            halo_copy(q).wait_send()

    for i in range(1, look + 1):
        @pl.when(k + i < n_ctx)
        def _():
            id_copy(i).wait_send()
            for h in range(halves):
                end_copy(i, h).wait_send()


def per_device(stream, seg_ids, mr_gain, mr_filter, li_gain, decay_rates, residues):
    rows, channels = stream.shape
    modes = decay_rates.shape[1]
    n_ctx, n_chan = lax.axis_size("ctx"), lax.axis_size("chan")
    assert rows == mr_filter.shape[1]
    longest = rows * n_ctx // 4
    look = max(1, min(n_ctx - 1, -(-(longest - 1) // rows)))
    tiles = channels // 128
    group = min(8, tiles)
    halves = tiles // group
    chunks = channels // min(512, channels)
    vmem = pl.BlockSpec(memory_space=pltpu.VMEM)
    dma = pltpu.SemaphoreType.DMA
    others = max(1, n_chan - 1)
    small = (8, 128)
    tables = [jnp.asarray(t) for t in dft_tables(rows)]
    operands = (
        stream, seg_ids.reshape(1, rows), mr_gain.reshape(1, channels), mr_filter,
        li_gain.reshape(1, channels), decay_rates.T, residues.T, *tables,
    )
    return pl.pallas_call(
        partial(kernel, n_ctx, n_chan, look, channels),
        out_shape=pltpu.VMEM((rows, channels), BF16),
        in_specs=[pl.BlockSpec(memory_space=pltpu.HBM)] * len(operands),
        out_specs=vmem,
        scratch_shapes=[pltpu.VMEM(x.shape, x.dtype) for x in operands]
        + [
            dma((len(operands),)),
            pltpu.VMEM((rows, channels), BF16),
            pltpu.VMEM((2 * rows, channels), BF16),
            pltpu.VMEM((2 * rows, channels), F32),
            pltpu.VMEM((rows, channels), BF16),
            pltpu.VMEM((tiles * (rows + PAD), 128), F32),
            pltpu.VMEM((tiles * (rows + PAD), 128), F32),
            pltpu.VMEM((tiles * modes, 128), F32),
            pltpu.VMEM((tiles * modes, 128), F32),
            pltpu.VMEM((rows, 128), F32),
            pltpu.VMEM((rows, 128), F32),
            pltpu.VMEM(small, F32),
            pltpu.VMEM(small, F32),
            pltpu.VMEM((others,) + small, F32),
            pltpu.VMEM((others,) + small, F32),
            pltpu.VMEM(small, F32),
            pltpu.VMEM(small, F32),
            pltpu.VMEM(small, F32),
            pltpu.VMEM((look,) + small, F32),
            pltpu.VMEM((halves, modes * group, 128), BF16),
            pltpu.VMEM((look * halves, modes * group, 128), BF16),
            dma((chunks,)), dma((chunks,)),
            dma((others,)), dma((others,)),
            dma((others,)), dma((others,)),
            dma, dma,
            dma((look,)), dma((look,)),
            dma((look * halves,)), dma((look * halves,)),
        ],
        compiler_params=pltpu.CompilerParams(
            collective_id=0, has_side_effects=True, vmem_limit_bytes=56 * 2**20
        ),
    )(*operands)


def solution(mesh):
    placed = (
        P("ctx", "chan"),
        P("ctx"),
        P("chan"),
        P("chan", None),
        P("chan"),
        P("chan", None),
        P("chan", None),
    )
    return jax.shard_map(
        per_device, mesh=mesh, in_specs=placed, out_specs=P("ctx", "chan"), check_vma=False
    )
```
